128 devices in a mesh: fsdp: 16 (over x, y), tp: 8 (over z, core).
Axes of the slice: x: 4, y: 4, z: 4, core: 2. Of those that a mesh axis runs over, the one named last changes fastest.
Arguments:
- grad: bfloat16 [4096, 16384], P('fsdp', 'tp'), may hold values from -34 to 34
- left_stat: float32 [8192, 8192], P('fsdp', 'tp'), may hold values from -0.75 to 3.2
- right_stat: float32 [8192, 8192], P('fsdp', 'tp'), may hold values from -0.75 to 3.2
- left_root: bfloat16 [8192, 8192], P('fsdp', 'tp'), may hold values from -0.65 to 2.2
- right_root: bfloat16 [8192, 8192], P('fsdp', 'tp'), may hold values from -0.65 to 2.2
- block_slot: int32 [8, 8], P('tp'), may hold values from 0 to 7, each once within a row
Outputs:
- new_left: float32 [8192, 8192], P('fsdp', 'tp')
- new_right: float32 [8192, 8192], P('fsdp', 'tp')
- update: bfloat16 [4096, 16384], P('fsdp', 'tp')
- grad_rms: float32 [], replicated
The draws below stay inside these ranges and needn't reach their ends.
Inputs may be any that keep to these rules, and one draw needn't show every extreme that they name: `block_slot`: row t names each slot of column group t once; each slot's matrix S of left_stat, right_stat, left_root and right_root is symmetric.
All inputs are finite; a program needn't handle non-finite values.
Results may differ from the reference program's by a relative error of at most 0.0058.
Values may be sent and summed in bfloat16 or wider, within the bound.
No kernel may reach another device: no remote copies, remote signals or barrier semaphores. Data moves between devices by JAX's collectives and lax.ppermute only.
A program may use at most 128 MiB of HBM per device.

```python
import math
import jax
import jax.numpy as jnp
from jax import lax

ROWS = 4096
COLS = 16384
BLOCK = 1024
HALF_BLOCK = 512
COL_BLOCKS = 2
COL_SLOTS = 8
SLOTS_PAIR = 1
STAT_ROWS = 8192
STAT_COLS = 8192
N_FSDP = 16
N_TP = 8


def symmetric_blocks(key, lowest, highest, spread):
    key_off, key_diag = jax.random.split(key)
    slot_count = N_FSDP // 2 * SLOTS_PAIR
    off_diagonal = jax.random.truncated_normal(key_off, -4.0, 4.0, (N_TP, slot_count, BLOCK, BLOCK), jnp.float32)
    off_diagonal = (off_diagonal + jnp.swapaxes(off_diagonal, 2, 3)) * (spread / math.sqrt(2.0 * BLOCK))
    diagonal = jax.random.uniform(key_diag, (N_TP, slot_count, BLOCK), jnp.float32, lowest, highest)
    identity = jnp.eye(BLOCK, dtype=jnp.float32)
    blocks = off_diagonal * (1.0 - identity) + diagonal[..., None] * identity
    shaped = blocks.reshape(N_TP, N_FSDP // 2, SLOTS_PAIR, 2, HALF_BLOCK, BLOCK)
    return shaped.transpose(1, 3, 2, 4, 0, 5).reshape(STAT_ROWS, STAT_COLS)


def draw_grad(key, part):
    key = jax.random.fold_in(key, 7)
    key_base, key_row, key_col, key_group = jax.random.split(key, 4)
    base_draw = jax.random.truncated_normal(key_base, -6.0, 6.0, (ROWS, COLS), jnp.float32)
    row_power = jax.random.uniform(key_row, (ROWS, 1), jnp.float32, 0.0, 1.0)
    grad_level = 0.01
    col_power = jax.random.uniform(key_col, (1, COLS), jnp.float32, 0.0, 1.0)
    hot_group = jax.random.randint(key_group, (), 0, N_TP)
    group_of = jnp.arange(COLS, dtype=jnp.int32) // (COLS // N_TP)
    group_boost = jnp.where(group_of == hot_group, 10.0 ** 0.5, 1.0).astype(jnp.float32)[None, :]
    row_trend = jnp.sqrt(1.0 + 2.0 * jnp.arange(ROWS, dtype=jnp.float32)[:, None] / ROWS)
    values = grad_level * base_draw * 10.0 ** row_power * 10.0 ** col_power * row_trend * group_boost
    return values.astype(jnp.bfloat16)


def draw_left_stat(key, part):
    key = jax.random.fold_in(key, 11)
    return symmetric_blocks(key, 1.0, 3.0, 0.7)


def draw_right_stat(key, part):
    key = jax.random.fold_in(key, 12)
    return symmetric_blocks(key, 1.0, 3.0, 0.7)


def draw_left_root(key, part):
    key = jax.random.fold_in(key, 13)
    return symmetric_blocks(key, 0.5, 2.0, 0.6).astype(jnp.bfloat16)


def draw_right_root(key, part):
    key = jax.random.fold_in(key, 14)
    return symmetric_blocks(key, 0.5, 2.0, 0.6).astype(jnp.bfloat16)


def setup_inputs(seed: int = 0) -> dict:
    arg_keys = jax.random.split(jax.random.key(seed), 7)
    grad = draw_grad(jax.random.fold_in(arg_keys[6], 71), 0)
    left_stat = draw_left_stat(jax.random.fold_in(arg_keys[6], 71), 0)
    right_stat = draw_right_stat(jax.random.fold_in(arg_keys[6], 71), 0)
    left_root = draw_left_root(jax.random.fold_in(arg_keys[6], 71), 0)
    right_root = draw_right_root(jax.random.fold_in(arg_keys[6], 71), 0)
    block_slot = jax.vmap(lambda own: jax.random.permutation(own, COL_SLOTS))(jax.random.split(arg_keys[5], N_TP)).reshape((N_TP, COL_SLOTS)).astype(jnp.int32)
    return {"grad": grad, "left_stat": left_stat, "right_stat": right_stat, "left_root": left_root, "right_root": right_root, "block_slot": block_slot}


ema_decay = 0.9
clip_level = 0.0625
norm_eps = 1e-06

def to_slots(statistic):
    shaped = statistic.reshape(N_FSDP // 2, 2, SLOTS_PAIR, HALF_BLOCK, N_TP, BLOCK)
    shaped = shaped.transpose(4, 0, 2, 1, 3, 5)
    return shaped.reshape(N_TP * COL_SLOTS, BLOCK, BLOCK)

def from_slots(slot_blocks):
    shaped = slot_blocks.reshape(N_TP, N_FSDP // 2, SLOTS_PAIR, 2, HALF_BLOCK, BLOCK)
    return shaped.transpose(1, 3, 2, 4, 0, 5).reshape(STAT_ROWS, STAT_COLS)

def to_blocks(matrix):
    shaped = matrix.reshape(ROWS // BLOCK, BLOCK, N_TP, COL_BLOCKS, BLOCK)
    return shaped.transpose(2, 0, 3, 1, 4).reshape(N_TP, COL_SLOTS, BLOCK, BLOCK)

def from_blocks(blocks):
    shaped = blocks.reshape(N_TP, ROWS // BLOCK, COL_BLOCKS, BLOCK, BLOCK)
    return shaped.transpose(1, 3, 0, 2, 4).reshape(ROWS, COLS)

def one_block(members):
    current, left_old, right_old, left_inv, right_inv = members
    gram_left = jnp.dot(current, current.T, preferred_element_type=jnp.float32)
    gram_right = jnp.dot(current.T, current, preferred_element_type=jnp.float32)
    left_new = ema_decay * left_old + (1.0 - ema_decay) * gram_left
    right_new = ema_decay * right_old + (1.0 - ema_decay) * gram_right
    partial_value = jnp.dot(left_inv, current, preferred_element_type=jnp.float32).astype(jnp.bfloat16)
    result = jnp.dot(partial_value, right_inv, preferred_element_type=jnp.float32).astype(jnp.bfloat16)
    return (left_new, right_new, result)

def reference(grad, left_stat, right_stat, left_root, right_root, block_slot):
    sum_squares = jnp.sum(jnp.square(grad.astype(jnp.float32)))
    grad_rms = jnp.sqrt(sum_squares / (ROWS * COLS) + norm_eps)
    factor = jnp.minimum(1.0, clip_level / grad_rms)
    clipped = (grad.astype(jnp.float32) * factor).astype(jnp.bfloat16)
    slot_ids = jnp.arange(COL_SLOTS, dtype=jnp.int32)
    holder = lax.optimization_barrier(jnp.sum(jnp.where(block_slot[:, None, :] == slot_ids[None, :, None], slot_ids[None, None, :], 0), axis=2)).astype(jnp.int32)
    by_slot = jnp.take_along_axis(to_blocks(clipped), holder[:, :, None, None], axis=1)
    members = (by_slot.reshape(N_TP * COL_SLOTS, BLOCK, BLOCK), to_slots(left_stat), to_slots(right_stat), to_slots(left_root), to_slots(right_root))
    left_new, right_new, update_slots = lax.map(one_block, members)
    update_blocks = jnp.take_along_axis(update_slots.reshape(N_TP, COL_SLOTS, BLOCK, BLOCK), block_slot[:, :, None, None].astype(jnp.int32), axis=1)
    return (from_slots(left_new), from_slots(right_new), from_blocks(update_blocks), grad_rms)
```

```python
import jax
import jax.numpy as jnp
from jax import lax
from jax.experimental import pallas as pl
from jax.experimental.pallas import tpu as pltpu
from jax.sharding import Mesh, PartitionSpec as P

ROWS = 4096
COLS = 16384
BLOCK = 1024
HALF = 512
NX = 4
NY = 4
PIECE = BLOCK // (NX * NY)


ema_decay = 0.9
clip_level = 0.0625
norm_eps = 1e-06

FSDP = ("x", "y")
VMEM = pl.BlockSpec(memory_space=pltpu.VMEM)
SMEM = pl.BlockSpec(memory_space=pltpu.SMEM)


def sum_over_all(value):
    for axis, bits in (("x", 2), ("y", 2), ("tp", 3)):
        for bit in range(bits):
            size = 2**bits
            pairs = [(source, source ^ (1 << bit)) for source in range(size)]
            value = value + lax.ppermute(value, axis, pairs)
    return value


def to_keepers_kernel(slot_ref, src_ref, dst_ref):
    for j in range(8):
        slot = slot_ref[0, j]
        x = slot // 2
        y = (slot % 2) * 2
        piece = src_ref[j // 2, :, (j % 2) * BLOCK : (j % 2 + 1) * BLOCK]
        dst_ref[y * NX + x] = piece
        dst_ref[(y + 1) * NX + x] = piece


def to_rows_kernel(slot_ref, src_ref, dst_ref):
    for j in range(8):
        slot = slot_ref[0, j]
        x = slot // 2
        y = (slot % 2) * 2
        for half in range(2):
            start = (j % 2) * BLOCK + half * HALF
            dst_ref[j // 2, :, start : start + HALF] = src_ref[(y + half) * NX + x]


def update_kernel(side_ref, factor_ref, g_ref, own_left_ref, other_left_ref, right_ref, out_ref, t_ref):
    tile = 256
    for i in range(BLOCK // tile):
        rows = slice(i * tile, (i + 1) * tile)
        t_ref[rows, :] = lax.dot_general(
            g_ref[rows, :], right_ref[...], (((1,), (1,)), ((), ())), preferred_element_type=jnp.float32
        ).astype(jnp.bfloat16)
    factor = factor_ref[0]
    per_tile = tile // PIECE
    for part, left_ref in ((0, own_left_ref), (1, other_left_ref)):
        base = (side_ref[0] ^ part) * (HALF // PIECE)
        for i in range(HALF // tile):
            rows = slice(i * tile, (i + 1) * tile)
            product = jnp.dot(left_ref[rows, :], t_ref[...], preferred_element_type=jnp.float32)
            product = (product * factor).astype(jnp.bfloat16)
            out_ref[pl.ds(base + i * per_tile, per_tile)] = product.reshape(per_tile, PIECE, HALF)


def per_device(grad, left_stat, right_stat, left_root, right_root, block_slot):
    side = lax.axis_index("y") % 2
    other_left = lax.ppermute(left_root, "y", [(i, i ^ 1) for i in range(NY)])
    local_sum = jnp.sum(jnp.square(grad.astype(jnp.float32)))
    sum_squares = sum_over_all(local_sum.reshape(1, 1))[0, 0]
    grad_rms = jnp.sqrt(sum_squares / (ROWS * COLS) + norm_eps)
    factor = jnp.minimum(1.0, clip_level / grad_rms)

    spread = lax.all_to_all(grad.reshape(NX, NX * PIECE // NX, 2 * BLOCK), "x", 0, 0)
    send = pl.pallas_call(
        to_keepers_kernel,
        out_shape=jax.ShapeDtypeStruct((NX * NY, PIECE, BLOCK), jnp.bfloat16),
        in_specs=[SMEM, VMEM],
        out_specs=VMEM,
    )(block_slot, spread)
    g = lax.all_to_all(send, ("y", "x"), 0, 0).reshape(BLOCK, BLOCK)

    out = pl.pallas_call(
        update_kernel,
        out_shape=jax.ShapeDtypeStruct((NX * NY, PIECE, HALF), jnp.bfloat16),
        in_specs=[SMEM, SMEM, VMEM, VMEM, VMEM, VMEM],
        out_specs=VMEM,
        scratch_shapes=[pltpu.VMEM((BLOCK, HALF), jnp.bfloat16)],
        compiler_params=pltpu.CompilerParams(vmem_limit_bytes=32 * 1024 * 1024),
    )(side.reshape(1), factor.reshape(1), g, left_root, other_left, right_root)
    back = lax.all_to_all(out, ("y", "x"), 0, 0)
    rows = pl.pallas_call(
        to_rows_kernel,
        out_shape=jax.ShapeDtypeStruct((NX, PIECE, 2 * BLOCK), jnp.bfloat16),
        in_specs=[SMEM, VMEM],
        out_specs=VMEM,
    )(block_slot, back)
    update = lax.all_to_all(rows, "x", 0, 0).reshape(grad.shape)

    scale = (1.0 - ema_decay) * factor * factor
    rows_half = lax.dynamic_slice_in_dim(g, side * HALF, HALF, 0)
    cols_half = lax.dynamic_slice_in_dim(g, side * HALF, HALF, 1)
    gram_left = lax.dot_general(
        rows_half, g, (((1,), (1,)), ((), ())), preferred_element_type=jnp.float32
    )
    gram_right = lax.dot_general(
        cols_half, g, (((0,), (0,)), ((), ())), preferred_element_type=jnp.float32
    )
    new_left = ema_decay * left_stat + scale * gram_left
    new_right = ema_decay * right_stat + scale * gram_right
    return (new_left, new_right, update, grad_rms)


def solution(mesh):
    grid = Mesh(mesh.devices.reshape(NX, NY, mesh.shape["tp"]), ("x", "y", "tp"))
    split = P(FSDP, "tp")
    return jax.shard_map(
        per_device,
        mesh=grid,
        in_specs=(split, split, split, split, split, P("tp", None)),
        out_specs=(split, split, split, P()),
        check_vma=False,
    )
```

```python
import jax
import jax.numpy as jnp
from jax import lax
from jax.experimental import pallas as pl
from jax.experimental.pallas import tpu as pltpu
from jax.sharding import Mesh, PartitionSpec as P

ROWS = 4096
COLS = 16384
BLOCK = 1024
HALF = 512
NX = 4
NY = 4
PIECE = BLOCK // (NX * NY)
PIECE_ROWS = PIECE * BLOCK // 128


ema_decay = 0.9
clip_level = 0.0625
norm_eps = 1e-06

FSDP = ("x", "y")
VMEM = pl.BlockSpec(memory_space=pltpu.VMEM)
ANY = pl.BlockSpec(memory_space=pl.ANY)
HBM = pl.BlockSpec(memory_space=pltpu.HBM)
SMEM = pl.BlockSpec(memory_space=pltpu.SMEM)


def add_partner(value, bit):
    return value + lax.ppermute(value, "tp", [(i, i ^ (1 << bit)) for i in range(8)])


def run_copies(pairs, sems):
    copies = [pltpu.make_async_copy(src, dst, sems.at[i]) for i, (src, dst) in enumerate(pairs)]
    for copy in copies:
        copy.start()
    for copy in copies:
        copy.wait()


def to_keepers_kernel(slot_ref, sum_ref, src_ref, dst_ref):
    total = jnp.broadcast_to(sum_ref[...], (16, 128))
    high = total.astype(jnp.bfloat16).astype(jnp.float32)
    middle = (total - high).astype(jnp.bfloat16).astype(jnp.float32)
    low = total - high - middle
    row = lax.broadcasted_iota(jnp.int32, (16, 128), 0)
    terms = jnp.where(row == 0, high, jnp.where(row == 1, middle, low)).astype(jnp.bfloat16)
    for keeper in range(NX * NY):
        dst_ref[keeper, PIECE_ROWS : PIECE_ROWS + 16, :] = terms
    for j in range(8):
        slot = slot_ref[0, j]
        keeper = (slot % 2) * 2 * NX + slot // 2
        for chunk in range(8):
            start = (j % 2) * BLOCK + chunk * 128
            part = src_ref[j // 2, :, start : start + 128]
            rows = slice(chunk * PIECE, (chunk + 1) * PIECE)
            dst_ref[keeper, rows, :] = part
            dst_ref[keeper + NX, rows, :] = part


def to_rows_kernel(slot_ref, src_ref, dst_ref, sems):
    pairs = []
    for j in range(8):
        slot = slot_ref[0, j]
        keeper = (slot % 2) * 2 * NX + slot // 2
        for half in range(2):
            start = (j % 2) * BLOCK + half * HALF
            pairs.append((src_ref.at[keeper + half * NX], dst_ref.at[j // 2, :, pl.ds(start, HALF)]))
    run_copies(pairs, sems)


def update_kernel(
    side_ref,
    pieces_ref,
    left_ref,
    corner_ref,
    right_ref,
    out_ref,
    g_ref,
    sum_ref,
    g_held,
    t_held,
    out_held,
    sems,
):
    tile = 256
    terms = pieces_ref[:, PIECE_ROWS:, :].astype(jnp.float32)
    sums = terms[:, 0, :] + terms[:, 1, :] + terms[:, 2, :]
    sum_ref[...] = jnp.sum(sums, axis=0, keepdims=True)[:, :1]
    for piece in range(NX * NY):
        for chunk in range(8):
            g_held[piece * PIECE : (piece + 1) * PIECE, chunk * 128 : (chunk + 1) * 128] = pieces_ref[
                piece, chunk * PIECE : (chunk + 1) * PIECE, :
            ]
    copies = [pltpu.make_async_copy(g_held, g_ref, sems.at[4])]
    copies[0].start()
    for i in range(BLOCK // tile):
        rows = slice(i * tile, (i + 1) * tile)
        t_held[rows, :] = lax.dot_general(
            g_held[rows, :], right_ref[...], (((1,), (1,)), ((), ())), preferred_element_type=jnp.float32
        ).astype(jnp.bfloat16)
    per_tile = tile // PIECE
    side = side_ref[0]
    own = pl.multiple_of(side * HALF, HALF)
    other = pl.multiple_of((1 - side) * HALF, HALF)
    t_own = t_held.at[pl.ds(own, HALF)]
    t_other = t_held.at[pl.ds(other, HALF)]
    for i in range(BLOCK // tile):
        part, inner = i // 2, i % 2
        rows = slice(inner * tile, (inner + 1) * tile)
        if part == 0:
            product = jnp.dot(left_ref[rows, :], t_held[...], preferred_element_type=jnp.float32)
            first = side * (HALF // PIECE) + inner * per_tile
        else:
            cross = left_ref[:, pl.ds(pl.multiple_of(other + inner * tile, tile), tile)]
            product = lax.dot_general(
                cross, t_own[...], (((0,), (0,)), ((), ())), preferred_element_type=jnp.float32
            ) + jnp.dot(corner_ref[rows, :], t_other[...], preferred_element_type=jnp.float32)
            first = (1 - side) * (HALF // PIECE) + inner * per_tile
        held = out_held.at[i * per_tile : (i + 1) * per_tile]
        held[...] = product.astype(jnp.bfloat16).reshape(per_tile, PIECE, HALF)
        copy = pltpu.make_async_copy(held, out_ref.at[pl.ds(first, per_tile)], sems.at[i])
        copy.start()
        copies.append(copy)
    for copy in copies:
        copy.wait()


def per_device(grad, left_stat, right_stat, left_root, right_root, block_slot):
    side = lax.axis_index("y") % 2
    corner = lax.dynamic_slice_in_dim(left_root, side * HALF, HALF, 1)
    other_corner = lax.ppermute(corner, "y", [(i, i ^ 1) for i in range(NY)])
    spread = lax.all_to_all(grad.reshape(NX, PIECE, 2 * BLOCK), "x", 0, 0)
    local_sum = jnp.sum(jnp.square(grad.astype(jnp.float32)))
    group_sum = add_partner(add_partner(local_sum.reshape(1, 1), 0), 1)
    spread, other_corner, group_sum = lax.optimization_barrier((spread, other_corner, group_sum))

    send = pl.pallas_call(
        to_keepers_kernel,
        out_shape=jax.ShapeDtypeStruct((NX * NY, PIECE_ROWS + 16, 128), jnp.bfloat16),
        in_specs=[SMEM, VMEM, VMEM],
        out_specs=VMEM,
        compiler_params=pltpu.CompilerParams(vmem_limit_bytes=16 * 1024 * 1024),
    )(block_slot, group_sum, spread)
    pieces = lax.all_to_all(send, ("y", "x"), 0, 0)

    out, g, half_sum = pl.pallas_call(
        update_kernel,
        out_shape=(
            pltpu.HBM((NX * NY, PIECE, HALF), jnp.bfloat16),
            pltpu.HBM((BLOCK, BLOCK), jnp.bfloat16),
            jax.ShapeDtypeStruct((1, 1), jnp.float32),
        ),
        in_specs=[SMEM, VMEM, VMEM, VMEM, VMEM],
        out_specs=(HBM, HBM, VMEM),
        scratch_shapes=[
            pltpu.VMEM((BLOCK, BLOCK), jnp.bfloat16),
            pltpu.VMEM((BLOCK, HALF), jnp.bfloat16),
            pltpu.VMEM((NX * NY, PIECE, HALF), jnp.bfloat16),
            pltpu.SemaphoreType.DMA((5,)),
        ],
        compiler_params=pltpu.CompilerParams(vmem_limit_bytes=32 * 1024 * 1024),
    )(side.reshape(1), pieces, left_root, other_corner, right_root)
    back = lax.all_to_all(out, ("y", "x"), 0, 0)
    sum_squares = add_partner(half_sum, 2)[0, 0]
    grad_rms = jnp.sqrt(sum_squares / (ROWS * COLS) + norm_eps)
    factor = jnp.minimum(1.0, clip_level / grad_rms)
    scale = (1.0 - ema_decay) * factor * factor
    rows_half = lax.dynamic_slice_in_dim(g, side * HALF, HALF, 0)
    cols_half = lax.dynamic_slice_in_dim(g, side * HALF, HALF, 1)
    gram_left = lax.dot_general(
        rows_half, g, (((1,), (1,)), ((), ())), preferred_element_type=jnp.float32
    )
    gram_right = lax.dot_general(
        cols_half, g, (((0,), (0,)), ((), ())), preferred_element_type=jnp.float32
    )
    new_left = ema_decay * left_stat + scale * gram_left
    new_right = ema_decay * right_stat + scale * gram_right
    back, new_left, new_right = lax.optimization_barrier((back, new_left, new_right))
    rows = pl.pallas_call(
        to_rows_kernel,
        out_shape=jax.ShapeDtypeStruct((NX, PIECE, 2 * BLOCK), jnp.bfloat16),
        in_specs=[SMEM, ANY],
        out_specs=ANY,
        scratch_shapes=[pltpu.SemaphoreType.DMA((16,))],
        compiler_params=pltpu.CompilerParams(vmem_limit_bytes=1024 * 1024),
    )(block_slot, back)
    update = lax.all_to_all(rows, "x", 0, 0).reshape(grad.shape)
    update = (update.astype(jnp.float32) * factor).astype(jnp.bfloat16)
    return (new_left, new_right, update, grad_rms)


def solution(mesh):
    grid = Mesh(mesh.devices.reshape(NX, NY, mesh.shape["tp"]), ("x", "y", "tp"))
    split = P(FSDP, "tp")
    return jax.shard_map(
        per_device,
        mesh=grid,
        in_specs=(split, split, split, split, split, P("tp", None)),
        out_specs=(split, split, split, P()),
        check_vma=False,
    )
```

```python
import jax
import jax.numpy as jnp
from jax import lax
from jax.experimental import pallas as pl
from jax.experimental.pallas import tpu as pltpu
from jax.sharding import Mesh, PartitionSpec as P

ROWS = 4096
COLS = 16384
BLOCK = 1024
HALF = 512
NX = 4
NY = 4
PIECE = BLOCK // (NX * NY)
PIECE_ROWS = PIECE * BLOCK // 128
SUM_SHAPE = (8, 128)


ema_decay = 0.9
clip_level = 0.0625
norm_eps = 1e-06

FSDP = ("x", "y")
VMEM = pl.BlockSpec(memory_space=pltpu.VMEM)
ANY = pl.BlockSpec(memory_space=pl.ANY)
HBM = pl.BlockSpec(memory_space=pltpu.HBM)
SMEM = pl.BlockSpec(memory_space=pltpu.SMEM)


def from_partner(value, bit):
    return lax.ppermute(value, "tp", [(i, i ^ (1 << bit)) for i in range(8)])


def square_sum_kernel(grad_ref, out_ref, held, sems):
    parts = 4
    rows = held.shape[0] // parts
    copies = []
    for i in range(parts):
        part = pl.ds(i * rows, rows)
        copies.append(pltpu.make_async_copy(grad_ref.at[part], held.at[part], sems.at[i]))
        copies[-1].start()
    total = jnp.zeros((8, held.shape[1]), jnp.float32)
    for i in range(parts):
        copies[i].wait()
        value = held[i * rows : (i + 1) * rows, :].astype(jnp.float32)
        total += jnp.sum((value * value).reshape(rows // 8, 8, held.shape[1]), axis=0)
    out_ref[...] = jnp.broadcast_to(jnp.sum(total).reshape(1, 1), out_ref.shape)


def run_copies(pairs, sems):
    copies = [pltpu.make_async_copy(src, dst, sems.at[i]) for i, (src, dst) in enumerate(pairs)]
    for copy in copies:
        copy.start()
    for copy in copies:
        copy.wait()


def to_keepers_kernel(slot_ref, own_ref, other_ref, src_ref, dst_ref):
    total = jnp.broadcast_to(own_ref[:1, :] + other_ref[:1, :], (16, 128))
    high = total.astype(jnp.bfloat16).astype(jnp.float32)
    middle = (total - high).astype(jnp.bfloat16).astype(jnp.float32)
    low = total - high - middle
    row = lax.broadcasted_iota(jnp.int32, (16, 128), 0)
    terms = jnp.where(row == 0, high, jnp.where(row == 1, middle, low)).astype(jnp.bfloat16)
    for keeper in range(NX * NY):
        dst_ref[keeper, PIECE_ROWS : PIECE_ROWS + 16, :] = terms
    for j in range(8):
        slot = slot_ref[0, j]
        keeper = (slot % 2) * 2 * NX + slot // 2
        for chunk in range(8):
            start = (j % 2) * BLOCK + chunk * 128
            part = src_ref[j // 2, :, start : start + 128]
            rows = slice(chunk * PIECE, (chunk + 1) * PIECE)
            dst_ref[keeper, rows, :] = part
            dst_ref[keeper + NX, rows, :] = part


def to_rows_kernel(slot_ref, src_ref, dst_ref, sems):
    pairs = []
    for j in range(8):
        slot = slot_ref[0, j]
        keeper = (slot % 2) * 2 * NX + slot // 2
        for half in range(2):
            start = (j % 2) * BLOCK + half * HALF
            pairs.append((src_ref.at[keeper + half * NX], dst_ref.at[j // 2, :, pl.ds(start, HALF)]))
    run_copies(pairs, sems)


def update_kernel(
    side_ref,
    pieces_ref,
    left_ref,
    corner_ref,
    right_ref,
    out_ref,
    g_ref,
    rms_ref,
    scale_ref,
    g_held,
    t_held,
    out_held,
    sems,
):
    tile = 256
    terms = pieces_ref[:, PIECE_ROWS:, :].astype(jnp.float32)
    sums = terms[:, 0, :] + terms[:, 1, :] + terms[:, 2, :]
    sum_squares = jnp.sum(sums, axis=0, keepdims=True)
    rms = jnp.sqrt(sum_squares / (ROWS * COLS) + norm_eps)
    factor = jnp.minimum(1.0, clip_level / rms)
    rms_ref[...] = jnp.broadcast_to(rms, rms_ref.shape)
    scale_ref[...] = jnp.tile((1.0 - ema_decay) * factor * factor, (8, BLOCK // 128))
    factor = jnp.tile(factor, (1, HALF // 128))
    for i in range(BLOCK // tile):
        for piece in range(i * tile // PIECE, (i + 1) * tile // PIECE):
            for chunk in range(8):
                g_held[piece * PIECE : (piece + 1) * PIECE, chunk * 128 : (chunk + 1) * 128] = pieces_ref[
                    piece, chunk * PIECE : (chunk + 1) * PIECE, :
                ]
        rows = slice(i * tile, (i + 1) * tile)
        t_held[rows, :] = lax.dot_general(
            g_held[rows, :], right_ref[...], (((1,), (1,)), ((), ())), preferred_element_type=jnp.float32
        ).astype(jnp.bfloat16)
    copies = [pltpu.make_async_copy(g_held, g_ref, sems.at[4])]
    copies[0].start()
    per_tile = tile // PIECE
    side = side_ref[0]
    own = pl.multiple_of(side * HALF, HALF)
    other = pl.multiple_of((1 - side) * HALF, HALF)
    t_own = t_held.at[pl.ds(own, HALF)]
    t_other = t_held.at[pl.ds(other, HALF)]
    for i in range(BLOCK // tile):
        part, inner = i // 2, i % 2
        rows = slice(inner * tile, (inner + 1) * tile)
        if part == 0:
            product = jnp.dot(left_ref[rows, :], t_held[...], preferred_element_type=jnp.float32)
            first = side * (HALF // PIECE) + inner * per_tile
        else:
            cross = left_ref[:, pl.ds(pl.multiple_of(other + inner * tile, tile), tile)]
            product = lax.dot_general(
                cross, t_own[...], (((0,), (0,)), ((), ())), preferred_element_type=jnp.float32
            ) + jnp.dot(corner_ref[rows, :], t_other[...], preferred_element_type=jnp.float32)
            first = (1 - side) * (HALF // PIECE) + inner * per_tile
        held = out_held.at[i * per_tile : (i + 1) * per_tile]
        held[...] = (product * factor).astype(jnp.bfloat16).reshape(per_tile, PIECE, HALF)
        copy = pltpu.make_async_copy(held, out_ref.at[pl.ds(first, per_tile)], sems.at[i])
        copy.start()
        copies.append(copy)
    for copy in copies:
        copy.wait()


def per_device(grad, left_stat, right_stat, left_root, right_root, block_slot):
    side = lax.axis_index("y") % 2
    corner = lax.dynamic_slice_in_dim(left_root, side * HALF, HALF, 1)
    other_corner = lax.ppermute(corner, "y", [(i, i ^ 1) for i in range(NY)])
    spread = lax.all_to_all(grad.reshape(NX, PIECE, 2 * BLOCK), "x", 0, 0)
    own_sum = pl.pallas_call(
        square_sum_kernel,
        out_shape=jax.ShapeDtypeStruct(SUM_SHAPE, jnp.float32),
        in_specs=[ANY],
        out_specs=VMEM,
        scratch_shapes=[pltpu.VMEM(grad.shape, jnp.bfloat16), pltpu.SemaphoreType.DMA((4,))],
    )(grad)
    own_sum += from_partner(own_sum, 0)
    own_sum += from_partner(own_sum, 1)
    other_sum = from_partner(own_sum, 2)
    spread, other_corner, own_sum, other_sum = lax.optimization_barrier(
        (spread, other_corner, own_sum, other_sum)
    )

    send = pl.pallas_call(
        to_keepers_kernel,
        out_shape=jax.ShapeDtypeStruct((NX * NY, PIECE_ROWS + 16, 128), jnp.bfloat16),
        in_specs=[SMEM, VMEM, VMEM, VMEM],
        out_specs=VMEM,
        compiler_params=pltpu.CompilerParams(vmem_limit_bytes=16 * 1024 * 1024),
    )(block_slot, own_sum, other_sum, spread)
    pieces = lax.all_to_all(send, ("y", "x"), 0, 0)

    out, g, rms, scale = pl.pallas_call(
        update_kernel,
        out_shape=(
            pltpu.HBM((NX * NY, PIECE, HALF), jnp.bfloat16),
            pltpu.HBM((BLOCK, BLOCK), jnp.bfloat16),
            jax.ShapeDtypeStruct(SUM_SHAPE, jnp.float32),
            jax.ShapeDtypeStruct((8, BLOCK), jnp.float32),
        ),
        in_specs=[SMEM, VMEM, VMEM, VMEM, VMEM],
        out_specs=(HBM, HBM, VMEM, VMEM),
        scratch_shapes=[
            pltpu.VMEM((BLOCK, BLOCK), jnp.bfloat16),
            pltpu.VMEM((BLOCK, HALF), jnp.bfloat16),
            pltpu.VMEM((NX * NY, PIECE, HALF), jnp.bfloat16),
            pltpu.SemaphoreType.DMA((5,)),
        ],
        compiler_params=pltpu.CompilerParams(vmem_limit_bytes=32 * 1024 * 1024),
    )(side.reshape(1), pieces, left_root, other_corner, right_root)
    back = lax.all_to_all(out, ("y", "x"), 0, 0)
    scale = scale[:1, :]
    rows_half = lax.dynamic_slice_in_dim(g, side * HALF, HALF, 0)
    cols_half = lax.dynamic_slice_in_dim(g, side * HALF, HALF, 1)
    gram_left = lax.dot_general(
        rows_half, g, (((1,), (1,)), ((), ())), preferred_element_type=jnp.float32
    )
    gram_right = lax.dot_general(
        cols_half, g, (((0,), (0,)), ((), ())), preferred_element_type=jnp.float32
    )
    new_left = ema_decay * left_stat + scale * gram_left
    new_right = ema_decay * right_stat + scale * gram_right
    grad_rms = rms[0, 0]
    back, new_left, new_right, grad_rms = lax.optimization_barrier((back, new_left, new_right, grad_rms))
    rows = pl.pallas_call(
        to_rows_kernel,
        out_shape=jax.ShapeDtypeStruct((NX, PIECE, 2 * BLOCK), jnp.bfloat16),
        in_specs=[SMEM, ANY],
        out_specs=ANY,
        scratch_shapes=[pltpu.SemaphoreType.DMA((16,))],
        compiler_params=pltpu.CompilerParams(vmem_limit_bytes=1024 * 1024),
    )(block_slot, back)
    update = lax.all_to_all(rows, "x", 0, 0).reshape(grad.shape)
    return (new_left, new_right, update, grad_rms)


def solution(mesh):
    grid = Mesh(mesh.devices.reshape(NX, NY, mesh.shape["tp"]), ("x", "y", "tp"))
    split = P(FSDP, "tp")
    return jax.shard_map(
        per_device,
        mesh=grid,
        in_specs=(split, split, split, split, split, P("tp", None)),
        out_specs=(split, split, split, P()),
        check_vma=False,
    )
```

```python
import jax
import jax.numpy as jnp
from jax import lax
from jax.experimental import pallas as pl
from jax.experimental.pallas import tpu as pltpu
from jax.sharding import Mesh, PartitionSpec as P

ROWS = 4096
COLS = 16384
BLOCK = 1024
HALF = 512
NX = 4
NY = 4
PIECE = BLOCK // (NX * NY)
PIECE_ROWS = PIECE * BLOCK // 128
SUM_SHAPE = (8, 128)


ema_decay = 0.9
clip_level = 0.0625
norm_eps = 1e-06

FSDP = ("x", "y")
VMEM = pl.BlockSpec(memory_space=pltpu.VMEM)
ANY = pl.BlockSpec(memory_space=pl.ANY)
HBM = pl.BlockSpec(memory_space=pltpu.HBM)
SMEM = pl.BlockSpec(memory_space=pltpu.SMEM)


def from_partner(value, bit):
    return lax.ppermute(value, "tp", [(i, i ^ (1 << bit)) for i in range(8)])


def square_sum_kernel(grad_ref, out_ref, held, sems):
    parts = 4
    rows = held.shape[0] // parts
    copies = []
    for i in range(parts):
        part = pl.ds(i * rows, rows)
        copies.append(pltpu.make_async_copy(grad_ref.at[part], held.at[part], sems.at[i]))
        copies[-1].start()
    total = jnp.zeros((8, held.shape[1]), jnp.float32)
    for i in range(parts):
        copies[i].wait()
        value = held[i * rows : (i + 1) * rows, :].astype(jnp.float32)
        total += jnp.sum((value * value).reshape(rows // 8, 8, held.shape[1]), axis=0)
    out_ref[...] = jnp.broadcast_to(jnp.sum(total).reshape(1, 1), out_ref.shape)


def to_keepers_kernel(slot_ref, own_ref, other_ref, src_ref, dst_ref):
    total = jnp.broadcast_to(own_ref[:1, :] + other_ref[:1, :], (16, 128))
    high = total.astype(jnp.bfloat16).astype(jnp.float32)
    middle = (total - high).astype(jnp.bfloat16).astype(jnp.float32)
    low = total - high - middle
    row = lax.broadcasted_iota(jnp.int32, (16, 128), 0)
    terms = jnp.where(row == 0, high, jnp.where(row == 1, middle, low)).astype(jnp.bfloat16)
    for keeper in range(NX * NY):
        dst_ref[keeper, PIECE_ROWS : PIECE_ROWS + 16, :] = terms
    for j in range(8):
        slot = slot_ref[0, j]
        keeper = (slot % 2) * 2 * NX + slot // 2
        for chunk in range(8):
            start = (j % 2) * BLOCK + chunk * 128
            part = src_ref[j // 2, :, start : start + 128]
            rows = slice(chunk * PIECE, (chunk + 1) * PIECE)
            dst_ref[keeper, rows, :] = part
            dst_ref[keeper + NX, rows, :] = part


def to_rows_kernel(slot_ref, src_ref, dst_ref):
    for j in range(8):
        slot = slot_ref[0, j]
        keeper = (slot % 2) * 2 * NX + slot // 2
        for half in range(2):
            start = (j % 2) * BLOCK + half * HALF
            dst_ref[j // 2, :, start : start + HALF] = src_ref[keeper + half * NX]


def update_kernel(
    side_ref,
    pieces_ref,
    left_ref,
    corner_ref,
    right_ref,
    out_ref,
    g_ref,
    rms_ref,
    scale_ref,
    g_held,
    t_held,
    out_held,
    sems,
):
    tile = 256
    terms = pieces_ref[:, PIECE_ROWS:, :].astype(jnp.float32)
    sums = terms[:, 0, :] + terms[:, 1, :] + terms[:, 2, :]
    sum_squares = jnp.sum(sums, axis=0, keepdims=True)
    rms = jnp.sqrt(sum_squares / (ROWS * COLS) + norm_eps)
    factor = jnp.minimum(1.0, clip_level / rms)
    rms_ref[...] = jnp.broadcast_to(rms, rms_ref.shape)
    scale_ref[...] = jnp.tile((1.0 - ema_decay) * factor * factor, (8, BLOCK // 128))
    factor = jnp.tile(factor, (1, HALF // 128))
    for i in range(BLOCK // tile):
        for piece in range(i * tile // PIECE, (i + 1) * tile // PIECE):
            for chunk in range(8):
                g_held[piece * PIECE : (piece + 1) * PIECE, chunk * 128 : (chunk + 1) * 128] = pieces_ref[
                    piece, chunk * PIECE : (chunk + 1) * PIECE, :
                ]
        rows = slice(i * tile, (i + 1) * tile)
        t_held[rows, :] = lax.dot_general(
            g_held[rows, :], right_ref[...], (((1,), (1,)), ((), ())), preferred_element_type=jnp.float32
        ).astype(jnp.bfloat16)
    copies = [pltpu.make_async_copy(g_held, g_ref, sems.at[4])]
    copies[0].start()
    per_tile = tile // PIECE
    side = side_ref[0]
    own = pl.multiple_of(side * HALF, HALF)
    other = pl.multiple_of((1 - side) * HALF, HALF)
    t_own = t_held.at[pl.ds(own, HALF)]
    t_other = t_held.at[pl.ds(other, HALF)]
    for i in range(BLOCK // tile):
        part, inner = i // 2, i % 2
        rows = slice(inner * tile, (inner + 1) * tile)
        if part == 0:
            product = jnp.dot(left_ref[rows, :], t_held[...], preferred_element_type=jnp.float32)
            first = side * (HALF // PIECE) + inner * per_tile
        else:
            cross = left_ref[:, pl.ds(pl.multiple_of(other + inner * tile, tile), tile)]
            product = lax.dot_general(
                cross, t_own[...], (((0,), (0,)), ((), ())), preferred_element_type=jnp.float32
            ) + jnp.dot(corner_ref[rows, :], t_other[...], preferred_element_type=jnp.float32)
            first = (1 - side) * (HALF // PIECE) + inner * per_tile
        held = out_held.at[i * per_tile : (i + 1) * per_tile]
        held[...] = (product * factor).astype(jnp.bfloat16).reshape(per_tile, PIECE, HALF)
        copy = pltpu.make_async_copy(held, out_ref.at[pl.ds(first, per_tile)], sems.at[i])
        copy.start()
        copies.append(copy)
    for copy in copies:
        copy.wait()


def per_device(grad, left_stat, right_stat, left_root, right_root, block_slot):
    side = lax.axis_index("y") % 2
    corner = lax.dynamic_slice_in_dim(left_root, side * HALF, HALF, 1)
    other_corner = lax.ppermute(corner, "y", [(i, i ^ 1) for i in range(NY)])
    spread = lax.all_to_all(grad.reshape(NX, PIECE, 2 * BLOCK), "x", 0, 0)
    own_sum = pl.pallas_call(
        square_sum_kernel,
        out_shape=jax.ShapeDtypeStruct(SUM_SHAPE, jnp.float32),
        in_specs=[ANY],
        out_specs=VMEM,
        scratch_shapes=[pltpu.VMEM(grad.shape, jnp.bfloat16), pltpu.SemaphoreType.DMA((4,))],
    )(grad)
    own_sum += from_partner(own_sum, 0)
    own_sum += from_partner(own_sum, 1)
    other_sum = from_partner(own_sum, 2)
    spread, other_corner, own_sum, other_sum = lax.optimization_barrier(
        (spread, other_corner, own_sum, other_sum)
    )

    send = pl.pallas_call(
        to_keepers_kernel,
        out_shape=jax.ShapeDtypeStruct((NX * NY, PIECE_ROWS + 16, 128), jnp.bfloat16),
        in_specs=[SMEM, VMEM, VMEM, VMEM],
        out_specs=VMEM,
        compiler_params=pltpu.CompilerParams(vmem_limit_bytes=16 * 1024 * 1024),
    )(block_slot, own_sum, other_sum, spread)
    pieces = lax.all_to_all(send, ("y", "x"), 0, 0)

    out, g, rms, scale = pl.pallas_call(
        update_kernel,
        out_shape=(
            pltpu.HBM((NX * NY, PIECE, HALF), jnp.bfloat16),
            pltpu.HBM((BLOCK, BLOCK), jnp.bfloat16),
            jax.ShapeDtypeStruct(SUM_SHAPE, jnp.float32),
            jax.ShapeDtypeStruct((8, BLOCK), jnp.float32),
        ),
        in_specs=[SMEM, VMEM, VMEM, VMEM, VMEM],
        out_specs=(HBM, HBM, VMEM, VMEM),
        scratch_shapes=[
            pltpu.VMEM((BLOCK, BLOCK), jnp.bfloat16),
            pltpu.VMEM((BLOCK, HALF), jnp.bfloat16),
            pltpu.VMEM((NX * NY, PIECE, HALF), jnp.bfloat16),
            pltpu.SemaphoreType.DMA((5,)),
        ],
        compiler_params=pltpu.CompilerParams(vmem_limit_bytes=32 * 1024 * 1024),
    )(side.reshape(1), pieces, left_root, other_corner, right_root)
    back = lax.all_to_all(out, ("y", "x"), 0, 0)
    scale = scale[:1, :]
    rows_half = lax.dynamic_slice_in_dim(g, side * HALF, HALF, 0)
    cols_half = lax.dynamic_slice_in_dim(g, side * HALF, HALF, 1)
    gram_left = lax.dot_general(
        rows_half, g, (((1,), (1,)), ((), ())), preferred_element_type=jnp.float32
    )
    gram_right = lax.dot_general(
        cols_half, g, (((0,), (0,)), ((), ())), preferred_element_type=jnp.float32
    )
    new_left = ema_decay * left_stat + scale * gram_left
    new_right = ema_decay * right_stat + scale * gram_right
    grad_rms = rms[0, 0]
    back, new_left, new_right, grad_rms = lax.optimization_barrier((back, new_left, new_right, grad_rms))
    rows = pl.pallas_call(
        to_rows_kernel,
        out_shape=jax.ShapeDtypeStruct((NX, PIECE, 2 * BLOCK), jnp.bfloat16),
        in_specs=[SMEM, VMEM],
        out_specs=VMEM,
        compiler_params=pltpu.CompilerParams(vmem_limit_bytes=8 * 1024 * 1024),
    )(block_slot, back)
    update = lax.all_to_all(rows, "x", 0, 0).reshape(grad.shape)
    return (new_left, new_right, update, grad_rms)


def solution(mesh):
    grid = Mesh(mesh.devices.reshape(NX, NY, mesh.shape["tp"]), ("x", "y", "tp"))
    split = P(FSDP, "tp")
    return jax.shard_map(
        per_device,
        mesh=grid,
        in_specs=(split, split, split, split, split, P("tp", None)),
        out_specs=(split, split, split, P()),
        check_vma=False,
    )
```

```python
import jax
import jax.numpy as jnp
from jax import lax
from jax.experimental import pallas as pl
from jax.experimental.pallas import tpu as pltpu
from jax.sharding import Mesh, PartitionSpec as P

ROWS = 4096
COLS = 16384
BLOCK = 1024
HALF = 512
NX = 4
NY = 4
PIECE = BLOCK // (NX * NY)
PIECE_ROWS = PIECE * BLOCK // 128
SUM_SHAPE = (8, 128)


ema_decay = 0.9
clip_level = 0.0625
norm_eps = 1e-06

FSDP = ("x", "y")
VMEM = pl.BlockSpec(memory_space=pltpu.VMEM)
ANY = pl.BlockSpec(memory_space=pl.ANY)
HBM = pl.BlockSpec(memory_space=pltpu.HBM)
SMEM = pl.BlockSpec(memory_space=pltpu.SMEM)


def from_partner(value, bit):
    return lax.ppermute(value, "tp", [(i, i ^ (1 << bit)) for i in range(8)])


def square_sum_kernel(grad_ref, out_ref):
    rows = 64
    total = jnp.zeros((8, grad_ref.shape[1]), jnp.float32)
    for first in range(0, grad_ref.shape[0], rows):
        value = grad_ref[first : first + rows, :].astype(jnp.float32)
        total += jnp.sum((value * value).reshape(rows // 8, 8, grad_ref.shape[1]), axis=0)
    out_ref[...] = jnp.broadcast_to(jnp.sum(total).reshape(1, 1), out_ref.shape)


def to_keepers_kernel(slot_ref, own_ref, other_ref, src_ref, dst_ref):
    total = jnp.broadcast_to(own_ref[:1, :] + other_ref[:1, :], (16, 128))
    high = total.astype(jnp.bfloat16).astype(jnp.float32)
    middle = (total - high).astype(jnp.bfloat16).astype(jnp.float32)
    low = total - high - middle
    row = lax.broadcasted_iota(jnp.int32, (16, 128), 0)
    terms = jnp.where(row == 0, high, jnp.where(row == 1, middle, low)).astype(jnp.bfloat16)
    for keeper in range(NX * NY):
        dst_ref[keeper, PIECE_ROWS : PIECE_ROWS + 16, :] = terms
    for j in range(8):
        slot = slot_ref[0, j]
        keeper = (slot % 2) * 2 * NX + slot // 2
        for chunk in range(8):
            start = (j % 2) * BLOCK + chunk * 128
            part = src_ref[j // 2, :, start : start + 128]
            rows = slice(chunk * PIECE, (chunk + 1) * PIECE)
            dst_ref[keeper, rows, :] = part
            dst_ref[keeper + NX, rows, :] = part


def to_rows_kernel(slot_ref, src_ref, dst_ref):
    for j in range(8):
        slot = slot_ref[0, j]
        keeper = (slot % 2) * 2 * NX + slot // 2
        for half in range(2):
            start = (j % 2) * BLOCK + half * HALF
            dst_ref[j // 2, :, start : start + HALF] = src_ref[keeper + half * NX]


def update_kernel(
    side_ref,
    pieces_ref,
    left_ref,
    corner_ref,
    right_ref,
    out_ref,
    g_ref,
    rms_ref,
    scale_ref,
    g_held,
    t_held,
    out_held,
    sems,
):
    tile = 256
    terms = pieces_ref[:, PIECE_ROWS:, :].astype(jnp.float32)
    sums = terms[:, 0, :] + terms[:, 1, :] + terms[:, 2, :]
    sum_squares = jnp.sum(sums, axis=0, keepdims=True)
    rms = jnp.sqrt(sum_squares / (ROWS * COLS) + norm_eps)
    factor = jnp.minimum(1.0, clip_level / rms)
    rms_ref[...] = jnp.broadcast_to(rms, rms_ref.shape)
    scale_ref[...] = jnp.tile((1.0 - ema_decay) * factor * factor, (8, BLOCK // 128))
    factor = jnp.tile(factor, (1, HALF // 128))
    for i in range(BLOCK // tile):
        for piece in range(i * tile // PIECE, (i + 1) * tile // PIECE):
            for chunk in range(8):
                g_held[piece * PIECE : (piece + 1) * PIECE, chunk * 128 : (chunk + 1) * 128] = pieces_ref[
                    piece, chunk * PIECE : (chunk + 1) * PIECE, :
                ]
        rows = slice(i * tile, (i + 1) * tile)
        t_held[rows, :] = lax.dot_general(
            g_held[rows, :], right_ref[...], (((1,), (1,)), ((), ())), preferred_element_type=jnp.float32
        ).astype(jnp.bfloat16)
    copies = [pltpu.make_async_copy(g_held, g_ref, sems.at[4])]
    copies[0].start()
    per_tile = tile // PIECE
    side = side_ref[0]
    own = pl.multiple_of(side * HALF, HALF)
    other = pl.multiple_of((1 - side) * HALF, HALF)
    t_own = t_held.at[pl.ds(own, HALF)]
    t_other = t_held.at[pl.ds(other, HALF)]
    for i in range(BLOCK // tile):
        part, inner = i // 2, i % 2
        rows = slice(inner * tile, (inner + 1) * tile)
        if part == 0:
            product = jnp.dot(left_ref[rows, :], t_held[...], preferred_element_type=jnp.float32)
            first = side * (HALF // PIECE) + inner * per_tile
        else:
            cross = left_ref[:, pl.ds(pl.multiple_of(other + inner * tile, tile), tile)]
            product = lax.dot_general(
                cross, t_own[...], (((0,), (0,)), ((), ())), preferred_element_type=jnp.float32
            ) + jnp.dot(corner_ref[rows, :], t_other[...], preferred_element_type=jnp.float32)
            first = (1 - side) * (HALF // PIECE) + inner * per_tile
        held = out_held.at[i * per_tile : (i + 1) * per_tile]
        held[...] = (product * factor).astype(jnp.bfloat16).reshape(per_tile, PIECE, HALF)
        copy = pltpu.make_async_copy(held, out_ref.at[pl.ds(first, per_tile)], sems.at[i])
        copy.start()
        copies.append(copy)
    for copy in copies:
        copy.wait()


def per_device(grad, left_stat, right_stat, left_root, right_root, block_slot):
    side = lax.axis_index("y") % 2
    corner = lax.dynamic_slice_in_dim(left_root, side * HALF, HALF, 1)
    other_corner = lax.ppermute(corner, "y", [(i, i ^ 1) for i in range(NY)])
    spread = lax.all_to_all(grad.reshape(NX, PIECE, 2 * BLOCK), "x", 0, 0)
    own_sum = pl.pallas_call(
        square_sum_kernel,
        out_shape=jax.ShapeDtypeStruct(SUM_SHAPE, jnp.float32),
        in_specs=[VMEM],
        out_specs=VMEM,
        compiler_params=pltpu.CompilerParams(vmem_limit_bytes=4 * 1024 * 1024),
    )(grad)
    own_sum += from_partner(own_sum, 0)
    own_sum += from_partner(own_sum, 1)
    other_sum = from_partner(own_sum, 2)
    spread, other_corner, own_sum, other_sum = lax.optimization_barrier(
        (spread, other_corner, own_sum, other_sum)
    )

    send = pl.pallas_call(
        to_keepers_kernel,
        out_shape=jax.ShapeDtypeStruct((NX * NY, PIECE_ROWS + 16, 128), jnp.bfloat16),
        in_specs=[SMEM, VMEM, VMEM, VMEM],
        out_specs=VMEM,
        compiler_params=pltpu.CompilerParams(vmem_limit_bytes=16 * 1024 * 1024),
    )(block_slot, own_sum, other_sum, spread)
    pieces = lax.all_to_all(send, ("y", "x"), 0, 0)

    out, g, rms, scale = pl.pallas_call(
        update_kernel,
        out_shape=(
            pltpu.HBM((NX * NY, PIECE, HALF), jnp.bfloat16),
            pltpu.HBM((BLOCK, BLOCK), jnp.bfloat16),
            jax.ShapeDtypeStruct(SUM_SHAPE, jnp.float32),
            jax.ShapeDtypeStruct((8, BLOCK), jnp.float32),
        ),
        in_specs=[SMEM, VMEM, VMEM, VMEM, VMEM],
        out_specs=(HBM, HBM, VMEM, VMEM),
        scratch_shapes=[
            pltpu.VMEM((BLOCK, BLOCK), jnp.bfloat16),
            pltpu.VMEM((BLOCK, HALF), jnp.bfloat16),
            pltpu.VMEM((NX * NY, PIECE, HALF), jnp.bfloat16),
            pltpu.SemaphoreType.DMA((5,)),
        ],
        compiler_params=pltpu.CompilerParams(vmem_limit_bytes=32 * 1024 * 1024),
    )(side.reshape(1), pieces, left_root, other_corner, right_root)
    back = lax.all_to_all(out, ("y", "x"), 0, 0)
    scale = scale[:1, :]
    rows_half = lax.dynamic_slice_in_dim(g, side * HALF, HALF, 0)
    cols_half = lax.dynamic_slice_in_dim(g, side * HALF, HALF, 1)
    gram_left = lax.dot_general(
        rows_half, g, (((1,), (1,)), ((), ())), preferred_element_type=jnp.float32
    )
    gram_right = lax.dot_general(
        cols_half, g, (((0,), (0,)), ((), ())), preferred_element_type=jnp.float32
    )
    new_left = ema_decay * left_stat + scale * gram_left
    new_right = ema_decay * right_stat + scale * gram_right
    grad_rms = rms[0, 0]
    back, new_left, new_right, grad_rms = lax.optimization_barrier((back, new_left, new_right, grad_rms))
    rows = pl.pallas_call(
        to_rows_kernel,
        out_shape=jax.ShapeDtypeStruct((NX, PIECE, 2 * BLOCK), jnp.bfloat16),
        in_specs=[SMEM, VMEM],
        out_specs=VMEM,
        compiler_params=pltpu.CompilerParams(vmem_limit_bytes=8 * 1024 * 1024),
    )(block_slot, back)
    update = lax.all_to_all(rows, "x", 0, 0).reshape(grad.shape)
    return (new_left, new_right, update, grad_rms)


def solution(mesh):
    grid = Mesh(mesh.devices.reshape(NX, NY, mesh.shape["tp"]), ("x", "y", "tp"))
    split = P(FSDP, "tp")
    return jax.shard_map(
        per_device,
        mesh=grid,
        in_specs=(split, split, split, split, split, P("tp", None)),
        out_specs=(split, split, split, P()),
        check_vma=False,
    )
```
